32 devices in a mesh: grp: 2 (over y), train: 4 (over z), test: 4 (over x, core).
Axes of the slice: x: 2, y: 2, z: 4, core: 2. Of those that a mesh axis runs over, the one named last changes fastest.
Arguments:
- test_features: bfloat16 [512, 16384], P('test', 'train'), may hold values from -6 to 6
- inverse_kernel: bfloat16 [16384, 16384], P('train', 'test'), may hold values from -0.046875 to 0.046875
- train_features: bfloat16 [2048, 16384], P(('grp', 'train'), 'test'), parts along dimension 0, may hold values from -0.046875 to 0.046875
Outputs:
- scores: float32 [512, 2048], P('test', ('grp', 'train')), parts along dimension 1
The draws below stay inside these ranges and needn't reach their ends.
There are 2 independent parts, one for each index of `grp`. The reference program is written for one: setup_inputs(seed, part) draws one part's arguments, and reference() takes and returns one part's arrays. A program takes and returns all parts, laid end to end along the dimension named above; an argument that names none is the same for every part. Nothing has to cross between parts.
All inputs are finite; a program needn't handle non-finite values.
Results may differ from the reference program's by a relative error of at most 0.0029.
Values may be sent and summed in bfloat16 or wider, within the bound.
A program may use at most 128 MiB of HBM per device.

```python
import jax
import jax.numpy as jnp
from jax import lax

P_SIZE = 16384
NTEST = 512
NTRAIN = 1024


def shard_levels(stream_key, dims, shards, smallest, largest):
    factor_of, own = 1.0, jax.random.fold_in(stream_key, 6)
    for position, shards_of in shards:
        draws = jnp.exp(jax.random.uniform(jax.random.fold_in(own, position), (shards_of,), jnp.float32, smallest / len(shards), largest / len(shards)))
        factor_of = factor_of * jnp.repeat(draws, dims[position] // shards_of).reshape([-1 if axis == position else 1 for axis in range(len(dims))])
    return factor_of


def centred(key, shape, scale, bound, shards=(), held_as=jnp.bfloat16):
    loudness = shard_levels(key, shape, shards, -0.22, 0.18) if shards else 1.0
    array = jax.random.normal(key, shape, jnp.float32) * scale * loudness
    return jnp.minimum(jnp.maximum(array, -bound), bound).astype(held_as)


def setup_inputs(seed: int = 0, part: int = 0) -> dict:
    seeds = jax.random.split(jax.random.key(seed), 4)
    part_splits = jax.random.split(jax.random.fold_in(seeds[3], part), 4)
    return {
        "test_features": centred(seeds[0], (NTEST, P_SIZE), 1.0, 6.0, ((0, 4), (1, 4))),
        "inverse_kernel": centred(seeds[1], (P_SIZE, P_SIZE), P_SIZE ** -0.5, 0.046875, ((0, 4), (1, 4))),
        "train_features": centred(part_splits[2], (NTRAIN, P_SIZE), P_SIZE ** -0.5, 0.046875, ((0, 4), (1, 4))),
    }


def reference(test_features, inverse_kernel, train_features):
    width = inverse_kernel.shape[1]
    block = min(width, 1024)
    left = test_features.astype(jnp.float32)
    pieces = []
    for begin in range(0, width, block):
        columns = inverse_kernel[:, begin:begin + block].astype(jnp.float32)
        part = jnp.dot(left, columns, preferred_element_type=jnp.float32, precision=lax.Precision.HIGHEST)
        pieces.append(part.astype(jnp.bfloat16))
    conditioned = jnp.concatenate(pieces, axis=1)
    return lax.dot_general(conditioned, train_features, (((1,), (1,)), ((), ())), preferred_element_type=jnp.float32)
```

```python
import functools

import jax
import jax.numpy as jnp
from jax import lax
from jax.experimental import pallas as pl
from jax.experimental.pallas import tpu as pltpu
from jax.sharding import PartitionSpec as P

CORES = 2
WIDTH = 256
SKEW = 2
MESH = pl.DeviceIdType.MESH


def kernel(
    n_grp, n_train, n_test, width, skew,
    test_hbm, kernel_hbm, train_hbm, out_ref,
    test_v, kernel_v, train_v, part, arrived, cond, acc, acc_in,
    kernel_sem, train_sem, own_sem,
    test_send, test_recv, pair_send, pair_recv,
    sum_send, sum_recv, total_send, total_recv, grp_send, grp_recv,
    score_send, score_recv,
):
    grp, z, me = lax.axis_index("grp"), lax.axis_index("train"), lax.axis_index("test")
    nx = n_test // CORES
    x, core = me // CORES, lax.rem(me, CORES)
    half = test_hbm.shape[0] // n_grp
    block = CORES * half
    per_pass = kernel_hbm.shape[1] // (2 * width)
    chunks = nx * per_pass
    last = n_train - 1

    def device(h, c):
        return lax.rem(x + h + nx, nx) * CORES + c

    def columns(way, j):
        return pl.ds(pl.multiple_of((way * per_pass + j) * width, width), width)

    def kernel_copy(way, j):
        slot = way * per_pass + j
        return pltpu.make_async_copy(kernel_hbm.at[:, columns(way, j)], kernel_v.at[slot], kernel_sem.at[slot])

    train_copy = pltpu.make_async_copy(train_hbm, train_v, train_sem)
    own_rows = test_hbm.at[pl.ds(pl.multiple_of(grp * half, half), half)]
    own_slot = pl.ds(pl.multiple_of(core * half, half), half)
    own_copy = pltpu.make_async_copy(own_rows, test_v.at[0, own_slot], own_sem)

    own_copy.start()
    for j in range(min(2, per_pass)):
        for way in range(2):
            kernel_copy(way, j).start()
    train_copy.start()

    barrier = pltpu.get_barrier_semaphore()
    for step in range(1, n_test):
        pl.semaphore_signal(barrier, inc=1, device_id={"test": lax.rem(me + step, n_test)}, device_id_type=MESH)
    for step in range(1, n_grp):
        pl.semaphore_signal(barrier, inc=1, device_id={"grp": lax.rem(grp + step, n_grp)}, device_id_type=MESH)

    @pl.when(z > 0)
    def _():
        pl.semaphore_signal(barrier, inc=1, device_id={"train": z - 1}, device_id_type=MESH)

    @pl.when(z < last)
    def _():
        pl.semaphore_signal(barrier, inc=1, device_id={"train": z + 1}, device_id_type=MESH)

    acc[...] = jnp.zeros_like(acc)
    near = jnp.where(z > 0, 1, 0) + jnp.where(z < last, 1, 0)
    pl.semaphore_wait(barrier, n_test - 1 + n_grp - 1 + near)

    def test_copy(h):
        return pltpu.make_async_remote_copy(
            src_ref=own_rows, dst_ref=test_v.at[h, own_slot],
            send_sem=test_send.at[h], recv_sem=test_recv.at[h],
            device_id={"test": device(-h, core)}, device_id_type=MESH,
        )

    def pair_copy(h):
        return pltpu.make_async_remote_copy(
            src_ref=own_rows if h == 0 else test_v.at[h, own_slot], dst_ref=test_v.at[h, own_slot],
            send_sem=pair_send.at[h], recv_sem=pair_recv.at[h],
            device_id={"test": device(0, 1 - core)}, device_id_type=MESH,
        )

    pair_copy(0).start()
    for h in range(1, nx):
        test_copy(h).start()
    own_copy.wait()
    pair_copy(0).wait_recv()

    def sum_copy(way, q):
        return pltpu.make_async_remote_copy(
            src_ref=part.at[way, q], dst_ref=arrived.at[way, q],
            send_sem=sum_send.at[way, q], recv_sem=sum_recv.at[way, q],
            device_id={"train": jnp.minimum(z + 1, last) if way == 0 else jnp.maximum(z - 1, 0)},
            device_id_type=MESH,
        )

    my_rows = pl.ds(pl.multiple_of(grp * block, block), block)

    def total_copy(way, q):
        ref = cond.at[way, q, my_rows]
        return pltpu.make_async_remote_copy(
            src_ref=ref, dst_ref=ref,
            send_sem=total_send.at[way, q], recv_sem=total_recv.at[way, q],
            device_id={"train": jnp.maximum(z - 1, 0) if way == 0 else jnp.minimum(z + 1, last)},
            device_id_type=MESH,
        )

    def grp_copy(way, q, step):
        ref = cond.at[way, q, my_rows]
        return pltpu.make_async_remote_copy(
            src_ref=ref, dst_ref=ref,
            send_sem=grp_send.at[way, q, step], recv_sem=grp_recv.at[way, q, step],
            device_id={"grp": lax.rem(grp + step, n_grp)}, device_id_type=MESH,
        )

    def inside(q):
        return (q >= 0) & (q < chunks)

    def do_step(s, carry):
        for way in range(2):
            @pl.when(s + 2 < per_pass)
            def _():
                kernel_copy(way, s + 2).start()

        @pl.when(s == 1)
        def _():
            train_copy.wait()

        for h in range(1, nx):
            @pl.when(s == h * per_pass + skew * jnp.minimum(z, last - z))
            def _():
                test_copy(h).wait_recv()
                pair_copy(h).start()
                pair_copy(h).wait_recv()

        for way in range(2):
            place = z if way == 0 else last - z
            q = s - skew * place

            @pl.when(inside(q))
            def _():
                h, j = q // per_pass, lax.rem(q, per_pass)

                @pl.when(q < per_pass)
                def _():
                    kernel_copy(way, j).wait()

                part[way, q] = jnp.dot(
                    test_v[h], kernel_v[way * per_pass + j], preferred_element_type=jnp.float32
                )

        for way in range(2):
            place = z if way == 0 else last - z
            q = s - skew * place

            @pl.when(inside(q) & (place > 0))
            def _():
                sum_copy(way, q).wait_recv()
                part[way, q] += arrived[way, q]

            @pl.when(inside(q) & (place < last))
            def _():
                sum_copy(way, q).start()

            @pl.when(inside(q) & (place == last))
            def _():
                cond[way, q, my_rows] = part[way, q].astype(jnp.bfloat16)

        for way in range(2):
            place = z if way == 0 else last - z
            q = s - skew * (2 * last - place)

            @pl.when(inside(q) & (place < last))
            def _():
                total_copy(way, q).wait_recv()

            @pl.when(inside(q) & (place > 0))
            def _():
                total_copy(way, q).start()

            @pl.when(inside(q))
            def _():
                for step in range(1, n_grp):
                    grp_copy(way, q, step).start()

        for way in range(2):
            place = z if way == 0 else last - z
            q = s - skew * (2 * last - place) - skew

            @pl.when(inside(q))
            def _():
                h, j = q // per_pass, lax.rem(q, per_pass)
                for step in range(1, n_grp):
                    grp_copy(way, q, step).wait_recv()
                value = lax.dot_general(
                    cond[way, q], train_v[:, columns(way, j)],
                    (((1,), (1,)), ((), ())), preferred_element_type=jnp.float32,
                )
                for c in range(CORES):
                    for g in range(n_grp):
                        begin = g * block + c * half
                        acc[h, c, g] += value[begin:begin + half]

        return carry

    lax.fori_loop(0, chunks + skew * (2 * last + 1), do_step, 0)

    def score_copy(h, flip):
        c = lax.rem(core + flip, CORES)
        return pltpu.make_async_remote_copy(
            src_ref=acc.at[h, c], dst_ref=acc_in.at[h, flip],
            send_sem=score_send.at[h, flip], recv_sem=score_recv.at[h, flip],
            device_id={"test": device(h, c)}, device_id_type=MESH,
        )

    others = [(h, flip) for h in range(nx - 1, -1, -1) for flip in range(CORES) if (h, flip) != (0, 0)]
    for h, flip in others:
        score_copy(h, flip).start()

    pair_copy(0).wait_send()
    for h in range(1, nx):
        test_copy(h).wait_send()
        pair_copy(h).wait_send()

    def drain(q, carry):
        for way in range(2):
            place = z if way == 0 else last - z

            @pl.when(place < last)
            def _():
                sum_copy(way, q).wait_send()

            @pl.when(place > 0)
            def _():
                total_copy(way, q).wait_send()

            for step in range(1, n_grp):
                grp_copy(way, q, step).wait_send()
        return carry

    lax.fori_loop(0, chunks, drain, 0)

    for h, flip in reversed(others):
        score_copy(h, flip).wait_recv()
    for g in range(n_grp):
        value = acc[0, core, g]
        for h, flip in others:
            value = value + acc_in[h, flip, g]
        out_ref[g * half:(g + 1) * half] = value
    for h, flip in others:
        score_copy(h, flip).wait_send()


def on_device(sizes, test_features, inverse_kernel, train_features):
    n_grp, n_train, n_test = sizes
    nx = n_test // CORES
    rows, depth = test_features.shape
    half = rows // n_grp
    block = CORES * half
    width = min(WIDTH, inverse_kernel.shape[1] // 2)
    per_pass = inverse_kernel.shape[1] // (2 * width)
    chunks = nx * per_pass
    trains = train_features.shape[0]
    dma = pltpu.SemaphoreType.DMA
    return pl.pallas_call(
        functools.partial(kernel, n_grp, n_train, n_test, width, SKEW),
        out_shape=jax.ShapeDtypeStruct((rows, trains), jnp.float32),
        in_specs=[pl.BlockSpec(memory_space=pl.ANY)] * 3,
        out_specs=pl.BlockSpec(memory_space=pltpu.VMEM),
        scratch_shapes=[
            pltpu.VMEM((nx, block, depth), jnp.bfloat16),
            pltpu.VMEM((2 * per_pass, depth, width), jnp.bfloat16),
            pltpu.VMEM(train_features.shape, jnp.bfloat16),
            pltpu.VMEM((2, chunks, block, width), jnp.float32),
            pltpu.VMEM((2, chunks, block, width), jnp.float32),
            pltpu.VMEM((2, chunks, n_grp * block, width), jnp.bfloat16),
            pltpu.VMEM((nx, CORES, n_grp, half, trains), jnp.float32),
            pltpu.VMEM((nx, CORES, n_grp, half, trains), jnp.float32),
            dma((2 * per_pass,)), dma, dma,
            dma((nx,)), dma((nx,)), dma((nx,)), dma((nx,)),
            dma((2, chunks)), dma((2, chunks)),
            dma((2, chunks)), dma((2, chunks)),
            dma((2, chunks, n_grp)), dma((2, chunks, n_grp)),
            dma((nx, CORES)), dma((nx, CORES)),
        ],
        compiler_params=pltpu.CompilerParams(
            collective_id=0, has_side_effects=True, vmem_limit_bytes=60 * 1024 * 1024
        ),
        cost_estimate=pl.CostEstimate(
            flops=2 * nx * block * depth * inverse_kernel.shape[1],
            bytes_accessed=2 * depth * inverse_kernel.shape[1], transcendentals=0,
        ),
    )(test_features, inverse_kernel, train_features)


def solution(mesh):
    sizes = tuple(mesh.shape[axis] for axis in ("grp", "train", "test"))
    return jax.shard_map(
        functools.partial(on_device, sizes),
        mesh=mesh,
        in_specs=(P("test", "train"), P("train", "test"), P(("grp", "train"), "test")),
        out_specs=P("test", ("grp", "train")),
        check_vma=False,
    )
```

```python
import functools

import jax
import jax.numpy as jnp
from jax import lax
from jax.experimental import pallas as pl
from jax.experimental.pallas import tpu as pltpu
from jax.sharding import PartitionSpec as P

CORES = 2
WIDTH = 256
SKEW = 2
MESH = pl.DeviceIdType.MESH


def kernel(
    n_grp, n_train, n_test, width, skew,
    test_hbm, kernel_hbm, train_hbm, out_ref,
    test_v, kernel_v, train_v, part, arrived, cond, acc, acc_in,
    kernel_sem, train_sem, own_sem,
    test_send, test_recv, pair_send, pair_recv,
    sum_send, sum_recv, total_send, total_recv, grp_send, grp_recv,
    score_send, score_recv,
):
    grp, z, me = lax.axis_index("grp"), lax.axis_index("train"), lax.axis_index("test")
    nx = n_test // CORES
    x, core = me // CORES, lax.rem(me, CORES)
    half = test_hbm.shape[0] // n_grp
    block = CORES * half
    per_pass = kernel_hbm.shape[1] // (2 * width)
    chunks = nx * per_pass
    last = n_train - 1
    lead = max(1, per_pass // 2)
    middle = lead + (nx - 1) * per_pass

    def split(q):
        other = q - lead
        own = (q < lead) | (q >= middle)
        h = jnp.where(own, 0, 1 + other // per_pass)
        j = jnp.where(q < lead, q, jnp.where(own, other - (nx - 1) * per_pass + lead, lax.rem(other + per_pass, per_pass)))
        first = (q < lead) | ((h <= 1) & (q < lead + per_pass) & (j >= lead))
        return h, j, first

    def device(h, c):
        return lax.rem(x + h + nx, nx) * CORES + c

    def columns(way, j):
        return pl.ds(pl.multiple_of((way * per_pass + j) * width, width), width)

    def kernel_copy(way, j):
        slot = way * per_pass + j
        return pltpu.make_async_copy(kernel_hbm.at[:, columns(way, j)], kernel_v.at[slot], kernel_sem.at[slot])

    train_copy = pltpu.make_async_copy(train_hbm, train_v, train_sem)
    own_rows = test_hbm.at[pl.ds(pl.multiple_of(grp * half, half), half)]
    own_slot = pl.ds(pl.multiple_of(core * half, half), half)
    own_copy = pltpu.make_async_copy(own_rows, test_v.at[0, own_slot], own_sem)

    own_copy.start()
    for j in range(min(2, per_pass)):
        for way in range(2):
            kernel_copy(way, j).start()

    barrier = pltpu.get_barrier_semaphore()
    for step in range(1, n_test):
        pl.semaphore_signal(barrier, inc=1, device_id={"test": lax.rem(me + step, n_test)}, device_id_type=MESH)
    for step in range(1, n_grp):
        pl.semaphore_signal(barrier, inc=1, device_id={"grp": lax.rem(grp + step, n_grp)}, device_id_type=MESH)

    @pl.when(z > 0)
    def _():
        pl.semaphore_signal(barrier, inc=1, device_id={"train": z - 1}, device_id_type=MESH)

    @pl.when(z < last)
    def _():
        pl.semaphore_signal(barrier, inc=1, device_id={"train": z + 1}, device_id_type=MESH)

    acc[...] = jnp.zeros_like(acc)
    near = jnp.where(z > 0, 1, 0) + jnp.where(z < last, 1, 0)
    pl.semaphore_wait(barrier, n_test - 1 + n_grp - 1 + near)

    def test_copy(h):
        return pltpu.make_async_remote_copy(
            src_ref=own_rows, dst_ref=test_v.at[h, own_slot],
            send_sem=test_send.at[h], recv_sem=test_recv.at[h],
            device_id={"test": device(-h, core)}, device_id_type=MESH,
        )

    def pair_copy(h):
        return pltpu.make_async_remote_copy(
            src_ref=own_rows if h == 0 else test_v.at[h, own_slot], dst_ref=test_v.at[h, own_slot],
            send_sem=pair_send.at[h], recv_sem=pair_recv.at[h],
            device_id={"test": device(0, 1 - core)}, device_id_type=MESH,
        )

    pair_copy(0).start()
    for h in range(1, nx):
        test_copy(h).start()
    own_copy.wait()
    pair_copy(0).wait_recv()

    def sum_copy(way, q):
        return pltpu.make_async_remote_copy(
            src_ref=part.at[way, q], dst_ref=arrived.at[way, q],
            send_sem=sum_send.at[way, q], recv_sem=sum_recv.at[way, q],
            device_id={"train": jnp.minimum(z + 1, last) if way == 0 else jnp.maximum(z - 1, 0)},
            device_id_type=MESH,
        )

    my_rows = pl.ds(pl.multiple_of(grp * block, block), block)

    def total_copy(way, q):
        ref = cond.at[way, q, my_rows]
        return pltpu.make_async_remote_copy(
            src_ref=ref, dst_ref=ref,
            send_sem=total_send.at[way, q], recv_sem=total_recv.at[way, q],
            device_id={"train": jnp.maximum(z - 1, 0) if way == 0 else jnp.minimum(z + 1, last)},
            device_id_type=MESH,
        )

    def grp_copy(way, q, step):
        ref = cond.at[way, q, my_rows]
        return pltpu.make_async_remote_copy(
            src_ref=ref, dst_ref=ref,
            send_sem=grp_send.at[way, q, step], recv_sem=grp_recv.at[way, q, step],
            device_id={"grp": lax.rem(grp + step, n_grp)}, device_id_type=MESH,
        )

    def inside(q):
        return (q >= 0) & (q < chunks)

    def score_copy(h, flip):
        c = lax.rem(core + flip, CORES)
        return pltpu.make_async_remote_copy(
            src_ref=acc.at[h, c], dst_ref=acc_in.at[h, flip],
            send_sem=score_send.at[h, flip], recv_sem=score_recv.at[h, flip],
            device_id={"test": device(h, c)}, device_id_type=MESH,
        )

    far = [(h, flip) for h in range(1, nx) for flip in range(CORES)]
    others = far + [(0, 1)]

    def do_step(s, carry):
        for way in range(2):
            @pl.when(s + 2 < per_pass)
            def _():
                kernel_copy(way, s + 2).start()

        @pl.when(s == 1)
        def _():
            train_copy.start()

        @pl.when(s == 2 * skew)
        def _():
            train_copy.wait()

        for h in range(1, nx):
            @pl.when(s == lead + (h - 1) * per_pass + skew * jnp.minimum(z, last - z))
            def _():
                test_copy(h).wait_recv()
                pair_copy(h).start()
                pair_copy(h).wait_recv()

        for way in range(2):
            place = z if way == 0 else last - z
            q = s - skew * place

            @pl.when(inside(q))
            def _():
                h, j, first = split(q)

                @pl.when(first)
                def _():
                    kernel_copy(way, j).wait()

                part[way, q] = jnp.dot(
                    test_v[h], kernel_v[way * per_pass + j], preferred_element_type=jnp.float32
                )

        for way in range(2):
            place = z if way == 0 else last - z
            q = s - skew * place

            @pl.when(inside(q) & (place > 0))
            def _():
                sum_copy(way, q).wait_recv()
                part[way, q] += arrived[way, q]

            @pl.when(inside(q) & (place < last))
            def _():
                sum_copy(way, q).start()

            @pl.when(inside(q) & (place == last))
            def _():
                cond[way, q, my_rows] = part[way, q].astype(jnp.bfloat16)

        for way in range(2):
            place = z if way == 0 else last - z
            q = s - skew * (2 * last - place)

            @pl.when(inside(q) & (place < last))
            def _():
                total_copy(way, q).wait_recv()

            @pl.when(inside(q) & (place > 0))
            def _():
                total_copy(way, q).start()

            @pl.when(inside(q))
            def _():
                for step in range(1, n_grp):
                    grp_copy(way, q, step).start()

        for way in range(2):
            place = z if way == 0 else last - z
            q = s - skew * (2 * last - place) - skew

            @pl.when(inside(q))
            def _():
                h, j, _ = split(q)
                for step in range(1, n_grp):
                    grp_copy(way, q, step).wait_recv()
                value = lax.dot_general(
                    cond[way, q], train_v[:, columns(way, j)],
                    (((1,), (1,)), ((), ())), preferred_element_type=jnp.float32,
                )
                for c in range(CORES):
                    for g in range(n_grp):
                        begin = g * block + c * half
                        acc[h, c, g] += value[begin:begin + half]

        @pl.when(s == middle - 1 + skew * (jnp.maximum(2 * last - z, last + z) + 1))
        def _():
            for h, flip in far:
                score_copy(h, flip).start()

        return carry

    lax.fori_loop(0, chunks + skew * (2 * last + 1), do_step, 0)
    score_copy(0, 1).start()

    pair_copy(0).wait_send()
    for h in range(1, nx):
        test_copy(h).wait_send()
        pair_copy(h).wait_send()

    def drain(q, carry):
        for way in range(2):
            place = z if way == 0 else last - z

            @pl.when(place < last)
            def _():
                sum_copy(way, q).wait_send()

            @pl.when(place > 0)
            def _():
                total_copy(way, q).wait_send()

            for step in range(1, n_grp):
                grp_copy(way, q, step).wait_send()
        return carry

    lax.fori_loop(0, chunks, drain, 0)

    for h, flip in others:
        score_copy(h, flip).wait_recv()
    for g in range(n_grp):
        value = acc[0, core, g]
        for h, flip in others:
            value = value + acc_in[h, flip, g]
        out_ref[g * half:(g + 1) * half] = value
    for h, flip in others:
        score_copy(h, flip).wait_send()


def on_device(sizes, test_features, inverse_kernel, train_features):
    n_grp, n_train, n_test = sizes
    nx = n_test // CORES
    rows, depth = test_features.shape
    half = rows // n_grp
    block = CORES * half
    width = min(WIDTH, inverse_kernel.shape[1] // 2)
    per_pass = inverse_kernel.shape[1] // (2 * width)
    chunks = nx * per_pass
    trains = train_features.shape[0]
    dma = pltpu.SemaphoreType.DMA
    return pl.pallas_call(
        functools.partial(kernel, n_grp, n_train, n_test, width, SKEW),
        out_shape=jax.ShapeDtypeStruct((rows, trains), jnp.float32),
        in_specs=[pl.BlockSpec(memory_space=pl.ANY)] * 3,
        out_specs=pl.BlockSpec(memory_space=pltpu.VMEM),
        scratch_shapes=[
            pltpu.VMEM((nx, block, depth), jnp.bfloat16),
            pltpu.VMEM((2 * per_pass, depth, width), jnp.bfloat16),
            pltpu.VMEM(train_features.shape, jnp.bfloat16),
            pltpu.VMEM((2, chunks, block, width), jnp.float32),
            pltpu.VMEM((2, chunks, block, width), jnp.float32),
            pltpu.VMEM((2, chunks, n_grp * block, width), jnp.bfloat16),
            pltpu.VMEM((nx, CORES, n_grp, half, trains), jnp.float32),
            pltpu.VMEM((nx, CORES, n_grp, half, trains), jnp.float32),
            dma((2 * per_pass,)), dma, dma,
            dma((nx,)), dma((nx,)), dma((nx,)), dma((nx,)),
            dma((2, chunks)), dma((2, chunks)),
            dma((2, chunks)), dma((2, chunks)),
            dma((2, chunks, n_grp)), dma((2, chunks, n_grp)),
            dma((nx, CORES)), dma((nx, CORES)),
        ],
        compiler_params=pltpu.CompilerParams(
            collective_id=0, has_side_effects=True, vmem_limit_bytes=60 * 1024 * 1024
        ),
        cost_estimate=pl.CostEstimate(
            flops=2 * nx * block * depth * inverse_kernel.shape[1],
            bytes_accessed=2 * depth * inverse_kernel.shape[1], transcendentals=0,
        ),
    )(test_features, inverse_kernel, train_features)


def solution(mesh):
    sizes = tuple(mesh.shape[axis] for axis in ("grp", "train", "test"))
    return jax.shard_map(
        functools.partial(on_device, sizes),
        mesh=mesh,
        in_specs=(P("test", "train"), P("train", "test"), P(("grp", "train"), "test")),
        out_specs=P("test", ("grp", "train")),
        check_vma=False,
    )
```

```python
import functools

import jax
import jax.numpy as jnp
from jax import lax
from jax.experimental import pallas as pl
from jax.experimental.pallas import tpu as pltpu
from jax.sharding import PartitionSpec as P

CORES = 2
WIDTH = 256
SKEW = 2
BACK = 2
SIDE = 4
MESH = pl.DeviceIdType.MESH


def kernel(
    n_grp, n_train, n_test, width, skew,
    test_hbm, kernel_hbm, train_hbm, out_ref,
    test_v, kernel_v, train_v, part, arrived, cond, acc, acc_in,
    kernel_sem, train_sem, own_sem,
    test_send, test_recv, pair_send, pair_recv,
    sum_send, sum_recv, total_send, total_recv, grp_send, grp_recv,
    score_send, score_recv,
):
    grp, z, me = lax.axis_index("grp"), lax.axis_index("train"), lax.axis_index("test")
    nx = n_test // CORES
    x, core = me // CORES, lax.rem(me, CORES)
    half = test_hbm.shape[0] // n_grp
    block = CORES * half
    per_pass = kernel_hbm.shape[1] // (2 * width)
    chunks = nx * per_pass
    last = n_train - 1
    lead = max(1, per_pass // 2)
    middle = lead + (nx - 1) * per_pass

    def split(q):
        other = q - lead
        own = (q < lead) | (q >= middle)
        h = jnp.where(own, 0, 1 + other // per_pass)
        j = jnp.where(q < lead, q, jnp.where(own, other - (nx - 1) * per_pass + lead, lax.rem(other + per_pass, per_pass)))
        first = (q < lead) | ((h <= 1) & (q < lead + per_pass) & (j >= lead))
        return h, j, first

    def device(h, c):
        return lax.rem(x + h + nx, nx) * CORES + c

    def columns(way, j):
        return pl.ds(pl.multiple_of((way * per_pass + j) * width, width), width)

    def kernel_copy(way, j):
        slot = way * per_pass + j
        return pltpu.make_async_copy(kernel_hbm.at[:, columns(way, j)], kernel_v.at[slot], kernel_sem.at[slot])

    train_copy = pltpu.make_async_copy(train_hbm, train_v, train_sem)
    own_rows = test_hbm.at[pl.ds(pl.multiple_of(grp * half, half), half)]
    own_slot = pl.ds(pl.multiple_of(core * half, half), half)
    own_copy = pltpu.make_async_copy(own_rows, test_v.at[0, own_slot], own_sem)

    own_copy.start()
    for j in range(min(2, per_pass)):
        for way in range(2):
            kernel_copy(way, j).start()

    barrier = pltpu.get_barrier_semaphore()
    for step in range(1, n_test):
        pl.semaphore_signal(barrier, inc=1, device_id={"test": lax.rem(me + step, n_test)}, device_id_type=MESH)
    for step in range(1, n_grp):
        pl.semaphore_signal(barrier, inc=1, device_id={"grp": lax.rem(grp + step, n_grp)}, device_id_type=MESH)

    @pl.when(z > 0)
    def _():
        pl.semaphore_signal(barrier, inc=1, device_id={"train": z - 1}, device_id_type=MESH)

    @pl.when(z < last)
    def _():
        pl.semaphore_signal(barrier, inc=1, device_id={"train": z + 1}, device_id_type=MESH)

    acc[...] = jnp.zeros_like(acc)
    near = jnp.where(z > 0, 1, 0) + jnp.where(z < last, 1, 0)
    pl.semaphore_wait(barrier, n_test - 1 + n_grp - 1 + near)

    def test_copy(h):
        return pltpu.make_async_remote_copy(
            src_ref=own_rows, dst_ref=test_v.at[h, own_slot],
            send_sem=test_send.at[h], recv_sem=test_recv.at[h],
            device_id={"test": device(-h, core)}, device_id_type=MESH,
        )

    def pair_copy(h):
        return pltpu.make_async_remote_copy(
            src_ref=own_rows if h == 0 else test_v.at[h, own_slot], dst_ref=test_v.at[h, own_slot],
            send_sem=pair_send.at[h], recv_sem=pair_recv.at[h],
            device_id={"test": device(0, 1 - core)}, device_id_type=MESH,
        )

    pair_copy(0).start()
    for h in range(1, nx):
        test_copy(h).start()
    own_copy.wait()
    pair_copy(0).wait_recv()

    def sum_copy(way, q):
        return pltpu.make_async_remote_copy(
            src_ref=part.at[way, q], dst_ref=arrived.at[way, q],
            send_sem=sum_send.at[way, q], recv_sem=sum_recv.at[way, q],
            device_id={"train": jnp.minimum(z + 1, last) if way == 0 else jnp.maximum(z - 1, 0)},
            device_id_type=MESH,
        )

    my_rows = pl.ds(pl.multiple_of(grp * block, block), block)

    def total_copy(way, q):
        ref = cond.at[way, q, my_rows]
        return pltpu.make_async_remote_copy(
            src_ref=ref, dst_ref=ref,
            send_sem=total_send.at[way, q], recv_sem=total_recv.at[way, q],
            device_id={"train": jnp.maximum(z - 1, 0) if way == 0 else jnp.minimum(z + 1, last)},
            device_id_type=MESH,
        )

    def grp_copy(way, q, step):
        ref = cond.at[way, q, my_rows]
        return pltpu.make_async_remote_copy(
            src_ref=ref, dst_ref=ref,
            send_sem=grp_send.at[way, q, step], recv_sem=grp_recv.at[way, q, step],
            device_id={"grp": lax.rem(grp + step, n_grp)}, device_id_type=MESH,
        )

    def inside(q):
        return (q >= 0) & (q < chunks)

    def score_copy(h, flip):
        c = lax.rem(core + flip, CORES)
        return pltpu.make_async_remote_copy(
            src_ref=acc.at[h, c], dst_ref=acc_in.at[h, flip],
            send_sem=score_send.at[h, flip], recv_sem=score_recv.at[h, flip],
            device_id={"test": device(h, c)}, device_id_type=MESH,
        )

    far = [(h, flip) for h in range(1, nx) for flip in range(CORES)]
    others = far + [(0, 1)]

    def do_step(s, carry):
        for way in range(2):
            @pl.when(s + 2 < per_pass)
            def _():
                kernel_copy(way, s + 2).start()

        @pl.when(s == 1)
        def _():
            train_copy.start()

        @pl.when(s == 2 * skew)
        def _():
            train_copy.wait()

        for h in range(1, nx):
            @pl.when(s == lead + (h - 1) * per_pass + skew * jnp.minimum(z, last - z))
            def _():
                test_copy(h).wait_recv()
                pair_copy(h).start()
                pair_copy(h).wait_recv()

        for way in range(2):
            place = z if way == 0 else last - z
            q = s - skew * place

            @pl.when(inside(q))
            def _():
                h, j, first = split(q)

                @pl.when(first)
                def _():
                    kernel_copy(way, j).wait()

                part[way, q] = jnp.dot(
                    test_v[h], kernel_v[way * per_pass + j], preferred_element_type=jnp.float32
                )

        for way in range(2):
            place = z if way == 0 else last - z
            q = s - skew * place

            @pl.when(inside(q) & (place > 0))
            def _():
                sum_copy(way, q).wait_recv()
                part[way, q] += arrived[way, q]

            @pl.when(inside(q) & (place < last))
            def _():
                sum_copy(way, q).start()

            @pl.when(inside(q) & (place == last))
            def _():
                cond[way, q, my_rows] = part[way, q].astype(jnp.bfloat16)

        for way in range(2):
            place = z if way == 0 else last - z
            q = s - skew * last - BACK * (last - place)

            @pl.when(inside(q) & (place < last))
            def _():
                total_copy(way, q).wait_recv()

            @pl.when(inside(q) & (place > 0))
            def _():
                total_copy(way, q).start()

            @pl.when(inside(q))
            def _():
                for step in range(1, n_grp):
                    grp_copy(way, q, step).start()

        for way in range(2):
            place = z if way == 0 else last - z
            q = s - skew * last - BACK * (last - place) - SIDE

            @pl.when(inside(q))
            def _():
                h, j, _ = split(q)
                for step in range(1, n_grp):
                    grp_copy(way, q, step).wait_recv()
                value = lax.dot_general(
                    cond[way, q], train_v[:, columns(way, j)],
                    (((1,), (1,)), ((), ())), preferred_element_type=jnp.float32,
                )
                for c in range(CORES):
                    for g in range(n_grp):
                        begin = g * block + c * half
                        acc[h, c, g] += value[begin:begin + half]

        @pl.when(s == middle - 1 + skew * last + BACK * jnp.maximum(last - z, z) + SIDE)
        def _():
            for h, flip in far:
                score_copy(h, flip).start()

        return carry

    lax.fori_loop(0, chunks + (skew + BACK) * last + SIDE, do_step, 0)
    score_copy(0, 1).start()

    pair_copy(0).wait_send()
    for h in range(1, nx):
        test_copy(h).wait_send()
        pair_copy(h).wait_send()

    def drain(q, carry):
        for way in range(2):
            place = z if way == 0 else last - z

            @pl.when(place < last)
            def _():
                sum_copy(way, q).wait_send()

            @pl.when(place > 0)
            def _():
                total_copy(way, q).wait_send()

            for step in range(1, n_grp):
                grp_copy(way, q, step).wait_send()
        return carry

    lax.fori_loop(0, chunks, drain, 0)

    for h, flip in others:
        score_copy(h, flip).wait_recv()
    for g in range(n_grp):
        value = acc[0, core, g]
        for h, flip in others:
            value = value + acc_in[h, flip, g]
        out_ref[g * half:(g + 1) * half] = value
    for h, flip in others:
        score_copy(h, flip).wait_send()


def on_device(sizes, test_features, inverse_kernel, train_features):
    n_grp, n_train, n_test = sizes
    nx = n_test // CORES
    rows, depth = test_features.shape
    half = rows // n_grp
    block = CORES * half
    width = min(WIDTH, inverse_kernel.shape[1] // 2)
    per_pass = inverse_kernel.shape[1] // (2 * width)
    chunks = nx * per_pass
    trains = train_features.shape[0]
    dma = pltpu.SemaphoreType.DMA
    return pl.pallas_call(
        functools.partial(kernel, n_grp, n_train, n_test, width, SKEW),
        out_shape=jax.ShapeDtypeStruct((rows, trains), jnp.float32),
        in_specs=[pl.BlockSpec(memory_space=pl.ANY)] * 3,
        out_specs=pl.BlockSpec(memory_space=pltpu.VMEM),
        scratch_shapes=[
            pltpu.VMEM((nx, block, depth), jnp.bfloat16),
            pltpu.VMEM((2 * per_pass, depth, width), jnp.bfloat16),
            pltpu.VMEM(train_features.shape, jnp.bfloat16),
            pltpu.VMEM((2, chunks, block, width), jnp.float32),
            pltpu.VMEM((2, chunks, block, width), jnp.float32),
            pltpu.VMEM((2, chunks, n_grp * block, width), jnp.bfloat16),
            pltpu.VMEM((nx, CORES, n_grp, half, trains), jnp.float32),
            pltpu.VMEM((nx, CORES, n_grp, half, trains), jnp.float32),
            dma((2 * per_pass,)), dma, dma,
            dma((nx,)), dma((nx,)), dma((nx,)), dma((nx,)),
            dma((2, chunks)), dma((2, chunks)),
            dma((2, chunks)), dma((2, chunks)),
            dma((2, chunks, n_grp)), dma((2, chunks, n_grp)),
            dma((nx, CORES)), dma((nx, CORES)),
        ],
        compiler_params=pltpu.CompilerParams(
            collective_id=0, has_side_effects=True, vmem_limit_bytes=60 * 1024 * 1024
        ),
        cost_estimate=pl.CostEstimate(
            flops=2 * nx * block * depth * inverse_kernel.shape[1],
            bytes_accessed=2 * depth * inverse_kernel.shape[1], transcendentals=0,
        ),
    )(test_features, inverse_kernel, train_features)


def solution(mesh):
    sizes = tuple(mesh.shape[axis] for axis in ("grp", "train", "test"))
    return jax.shard_map(
        functools.partial(on_device, sizes),
        mesh=mesh,
        in_specs=(P("test", "train"), P("train", "test"), P(("grp", "train"), "test")),
        out_specs=P("test", ("grp", "train")),
        check_vma=False,
    )
```

```python
import functools

import jax
import jax.numpy as jnp
from jax import lax
from jax.experimental import pallas as pl
from jax.experimental.pallas import tpu as pltpu
from jax.sharding import PartitionSpec as P

CORES = 2
WIDTH = 256
SKEW = 2
BACK = 2
SIDE = 4
MESH = pl.DeviceIdType.MESH


def kernel(
    n_grp, n_train, n_test, width, skew,
    test_hbm, kernel_hbm, train_hbm, out_ref,
    test_v, kernel_v, train_v, part, arrived, cond, acc, acc_in,
    kernel_sem, train_sem, own_sem,
    test_send, test_recv, pair_send, pair_recv,
    sum_send, sum_recv, total_send, total_recv, grp_send, grp_recv,
    score_send, score_recv,
):
    grp, z, me = lax.axis_index("grp"), lax.axis_index("train"), lax.axis_index("test")
    nx = n_test // CORES
    x, core = me // CORES, lax.rem(me, CORES)
    half = test_hbm.shape[0] // n_grp
    block = CORES * half
    per_pass = kernel_hbm.shape[1] // (2 * width)
    chunks = nx * per_pass
    last = n_train - 1
    lead = max(1, 5 * per_pass // 8)
    middle = lead + (nx - 1) * per_pass

    def split(q):
        other = q - lead
        own = (q < lead) | (q >= middle)
        h = jnp.where(own, 0, 1 + other // per_pass)
        j = jnp.where(q < lead, q, jnp.where(own, other - (nx - 1) * per_pass + lead, lax.rem(other + per_pass, per_pass)))
        first = (q < lead) | ((h <= 1) & (q < lead + per_pass) & (j >= lead))
        return h, j, first

    def device(h, c):
        return lax.rem(x + h + nx, nx) * CORES + c

    def columns(way, j):
        return pl.ds(pl.multiple_of((way * per_pass + j) * width, width), width)

    def kernel_copy(way, j):
        slot = way * per_pass + j
        return pltpu.make_async_copy(kernel_hbm.at[:, columns(way, j)], kernel_v.at[slot], kernel_sem.at[slot])

    train_copy = pltpu.make_async_copy(train_hbm, train_v, train_sem)
    own_rows = test_hbm.at[pl.ds(pl.multiple_of(grp * half, half), half)]
    own_slot = pl.ds(pl.multiple_of(core * half, half), half)
    own_copy = pltpu.make_async_copy(own_rows, test_v.at[0, own_slot], own_sem)

    own_copy.start()
    for j in range(min(2, per_pass)):
        for way in range(2):
            kernel_copy(way, j).start()

    barrier = pltpu.get_barrier_semaphore()
    for step in range(1, n_test):
        pl.semaphore_signal(barrier, inc=1, device_id={"test": lax.rem(me + step, n_test)}, device_id_type=MESH)
    for step in range(1, n_grp):
        pl.semaphore_signal(barrier, inc=1, device_id={"grp": lax.rem(grp + step, n_grp)}, device_id_type=MESH)

    @pl.when(z > 0)
    def _():
        pl.semaphore_signal(barrier, inc=1, device_id={"train": z - 1}, device_id_type=MESH)

    @pl.when(z < last)
    def _():
        pl.semaphore_signal(barrier, inc=1, device_id={"train": z + 1}, device_id_type=MESH)

    acc[...] = jnp.zeros_like(acc)
    near = jnp.where(z > 0, 1, 0) + jnp.where(z < last, 1, 0)
    pl.semaphore_wait(barrier, n_test - 1 + n_grp - 1 + near)

    def test_copy(h):
        return pltpu.make_async_remote_copy(
            src_ref=own_rows, dst_ref=test_v.at[h, own_slot],
            send_sem=test_send.at[h], recv_sem=test_recv.at[h],
            device_id={"test": device(-h, core)}, device_id_type=MESH,
        )

    def pair_copy(h):
        return pltpu.make_async_remote_copy(
            src_ref=own_rows if h == 0 else test_v.at[h, own_slot], dst_ref=test_v.at[h, own_slot],
            send_sem=pair_send.at[h], recv_sem=pair_recv.at[h],
            device_id={"test": device(0, 1 - core)}, device_id_type=MESH,
        )

    pair_copy(0).start()
    for h in range(1, nx):
        test_copy(h).start()
    own_copy.wait()
    pair_copy(0).wait_recv()

    def sum_copy(way, q):
        return pltpu.make_async_remote_copy(
            src_ref=part.at[way, q], dst_ref=arrived.at[way, q],
            send_sem=sum_send.at[way, q], recv_sem=sum_recv.at[way, q],
            device_id={"train": jnp.minimum(z + 1, last) if way == 0 else jnp.maximum(z - 1, 0)},
            device_id_type=MESH,
        )

    my_rows = pl.ds(pl.multiple_of(grp * block, block), block)

    def total_copy(way, q):
        ref = cond.at[way, q, my_rows]
        return pltpu.make_async_remote_copy(
            src_ref=ref, dst_ref=ref,
            send_sem=total_send.at[way, q], recv_sem=total_recv.at[way, q],
            device_id={"train": jnp.maximum(z - 1, 0) if way == 0 else jnp.minimum(z + 1, last)},
            device_id_type=MESH,
        )

    def grp_copy(way, q, step):
        ref = cond.at[way, q, my_rows]
        return pltpu.make_async_remote_copy(
            src_ref=ref, dst_ref=ref,
            send_sem=grp_send.at[way, q, step], recv_sem=grp_recv.at[way, q, step],
            device_id={"grp": lax.rem(grp + step, n_grp)}, device_id_type=MESH,
        )

    def inside(q):
        return (q >= 0) & (q < chunks)

    def score_copy(h, flip):
        c = lax.rem(core + flip, CORES)
        return pltpu.make_async_remote_copy(
            src_ref=acc.at[h, c], dst_ref=acc_in.at[h, flip],
            send_sem=score_send.at[h, flip], recv_sem=score_recv.at[h, flip],
            device_id={"test": device(h, c)}, device_id_type=MESH,
        )

    far = [(h, flip) for h in range(1, nx) for flip in range(CORES)]
    others = far + [(0, 1)]

    def do_step(s, carry):
        for way in range(2):
            @pl.when(s + 2 < per_pass)
            def _():
                kernel_copy(way, s + 2).start()

        @pl.when(s == 1)
        def _():
            train_copy.start()

        @pl.when(s == 2 * skew)
        def _():
            train_copy.wait()

        for h in range(1, nx):
            @pl.when(s == lead + (h - 1) * per_pass + skew * jnp.minimum(z, last - z))
            def _():
                test_copy(h).wait_recv()
                pair_copy(h).start()
                pair_copy(h).wait_recv()

        for way in range(2):
            place = z if way == 0 else last - z
            q = s - skew * place

            @pl.when(inside(q))
            def _():
                h, j, first = split(q)

                @pl.when(first)
                def _():
                    kernel_copy(way, j).wait()

                part[way, q] = jnp.dot(
                    test_v[h], kernel_v[way * per_pass + j], preferred_element_type=jnp.float32
                )

        for way in range(2):
            place = z if way == 0 else last - z
            q = s - skew * place

            @pl.when(inside(q) & (place > 0))
            def _():
                sum_copy(way, q).wait_recv()
                part[way, q] += arrived[way, q]

            @pl.when(inside(q) & (place < last))
            def _():
                sum_copy(way, q).start()

            @pl.when(inside(q) & (place == last))
            def _():
                cond[way, q, my_rows] = part[way, q].astype(jnp.bfloat16)

        for way in range(2):
            place = z if way == 0 else last - z
            q = s - skew * last - BACK * (last - place)

            @pl.when(inside(q) & (place < last))
            def _():
                total_copy(way, q).wait_recv()

            @pl.when(inside(q) & (place > 0))
            def _():
                total_copy(way, q).start()

            @pl.when(inside(q))
            def _():
                for step in range(1, n_grp):
                    grp_copy(way, q, step).start()

        for way in range(2):
            place = z if way == 0 else last - z
            q = s - skew * last - BACK * (last - place) - SIDE

            @pl.when(inside(q))
            def _():
                h, j, _ = split(q)
                for step in range(1, n_grp):
                    grp_copy(way, q, step).wait_recv()
                value = lax.dot_general(
                    cond[way, q], train_v[:, columns(way, j)],
                    (((1,), (1,)), ((), ())), preferred_element_type=jnp.float32,
                )
                for c in range(CORES):
                    for g in range(n_grp):
                        begin = g * block + c * half
                        acc[h, c, g] += value[begin:begin + half]

        @pl.when(s == middle - 1 + skew * last + BACK * jnp.maximum(last - z, z) + SIDE)
        def _():
            for h, flip in far:
                score_copy(h, flip).start()

        return carry

    lax.fori_loop(0, chunks + (skew + BACK) * last + SIDE, do_step, 0)
    score_copy(0, 1).start()

    pair_copy(0).wait_send()
    for h in range(1, nx):
        test_copy(h).wait_send()
        pair_copy(h).wait_send()

    def drain(q, carry):
        for way in range(2):
            place = z if way == 0 else last - z

            @pl.when(place < last)
            def _():
                sum_copy(way, q).wait_send()

            @pl.when(place > 0)
            def _():
                total_copy(way, q).wait_send()

            for step in range(1, n_grp):
                grp_copy(way, q, step).wait_send()
        return carry

    lax.fori_loop(0, chunks, drain, 0)

    for h, flip in others:
        score_copy(h, flip).wait_recv()
    for g in range(n_grp):
        value = acc[0, core, g]
        for h, flip in others:
            value = value + acc_in[h, flip, g]
        out_ref[g * half:(g + 1) * half] = value
    for h, flip in others:
        score_copy(h, flip).wait_send()


def on_device(sizes, test_features, inverse_kernel, train_features):
    n_grp, n_train, n_test = sizes
    nx = n_test // CORES
    rows, depth = test_features.shape
    half = rows // n_grp
    block = CORES * half
    width = min(WIDTH, inverse_kernel.shape[1] // 2)
    per_pass = inverse_kernel.shape[1] // (2 * width)
    chunks = nx * per_pass
    trains = train_features.shape[0]
    dma = pltpu.SemaphoreType.DMA
    return pl.pallas_call(
        functools.partial(kernel, n_grp, n_train, n_test, width, SKEW),
        out_shape=jax.ShapeDtypeStruct((rows, trains), jnp.float32),
        in_specs=[pl.BlockSpec(memory_space=pl.ANY)] * 3,
        out_specs=pl.BlockSpec(memory_space=pltpu.VMEM),
        scratch_shapes=[
            pltpu.VMEM((nx, block, depth), jnp.bfloat16),
            pltpu.VMEM((2 * per_pass, depth, width), jnp.bfloat16),
            pltpu.VMEM(train_features.shape, jnp.bfloat16),
            pltpu.VMEM((2, chunks, block, width), jnp.float32),
            pltpu.VMEM((2, chunks, block, width), jnp.float32),
            pltpu.VMEM((2, chunks, n_grp * block, width), jnp.bfloat16),
            pltpu.VMEM((nx, CORES, n_grp, half, trains), jnp.float32),
            pltpu.VMEM((nx, CORES, n_grp, half, trains), jnp.float32),
            dma((2 * per_pass,)), dma, dma,
            dma((nx,)), dma((nx,)), dma((nx,)), dma((nx,)),
            dma((2, chunks)), dma((2, chunks)),
            dma((2, chunks)), dma((2, chunks)),
            dma((2, chunks, n_grp)), dma((2, chunks, n_grp)),
            dma((nx, CORES)), dma((nx, CORES)),
        ],
        compiler_params=pltpu.CompilerParams(
            collective_id=0, has_side_effects=True, vmem_limit_bytes=60 * 1024 * 1024
        ),
        cost_estimate=pl.CostEstimate(
            flops=2 * nx * block * depth * inverse_kernel.shape[1],
            bytes_accessed=2 * depth * inverse_kernel.shape[1], transcendentals=0,
        ),
    )(test_features, inverse_kernel, train_features)


def solution(mesh):
    sizes = tuple(mesh.shape[axis] for axis in ("grp", "train", "test"))
    return jax.shard_map(
        functools.partial(on_device, sizes),
        mesh=mesh,
        in_specs=(P("test", "train"), P("train", "test"), P(("grp", "train"), "test")),
        out_specs=P("test", ("grp", "train")),
        check_vma=False,
    )
```
